32 devices in a mesh: dp: 16 (over z, x, core), tensor: 2 (over y).
Axes of the slice: x: 2, y: 2, z: 4, core: 2. Of those that a mesh axis runs over, the one named last changes fastest.
Arguments:
- x_hidden: bfloat16 [4096, 8192], P('dp', 'tensor'), may hold values from -6 to 6
- norm_gain: bfloat16 [8192], P('tensor'), may hold values from 0.25 to 1.75
- queries_upper: bfloat16 [4096, 4096], P('dp', 'tensor'), may hold values from -6 to 6
- block_key_value_above: bfloat16 [2, 4096, 1024], P(None, 'dp', 'tensor'), may hold values from -6 to 6
- out_grad_upper: bfloat16 [4096, 4096], P('dp', 'tensor'), may hold values from -6 to 6
- resid_grad: bfloat16 [4096, 8192], P('dp', 'tensor'), may hold values from -2 to 2
- queries_lower: bfloat16 [4096, 4096], P('dp', 'tensor'), may hold values from -6 to 6
- block_key_value_below: bfloat16 [2, 4096, 1024], P(None, 'dp', 'tensor'), may hold values from -6 to 6
- w_query: bfloat16 [8192, 4096], P('dp', 'tensor'), may hold values from -0.0625 to 0.0625
- key_weight_above: bfloat16 [8192, 1024], P('dp', 'tensor'), may hold values from -0.0625 to 0.0625
- value_weight_above: bfloat16 [8192, 1024], P('dp', 'tensor'), may hold values from -0.0625 to 0.0625
- w_output: bfloat16 [4096, 8192], P('tensor', 'dp'), may hold values from -0.09375 to 0.09375
- prefix_upper: bfloat16 [2, 2048, 1024], P(None, None, 'tensor'), may hold values from -6 to 6
- prefix_lower: bfloat16 [2, 2048, 1024], P(None, None, 'tensor'), may hold values from -6 to 6
- master: float32 [2, 2, 2048, 1024], P(None, None, 'dp', 'tensor'), may hold values from -6 to 6
- first_moment_state: float32 [2, 2, 2048, 1024], P(None, None, 'dp', 'tensor'), may hold values from -0.046875 to 0.046875
- second_moment_state: float32 [2, 2, 2048, 1024], P(None, None, 'dp', 'tensor'), may hold values from 0.0001 to 0.01
- offsets: int32 [16], P('dp'), may hold values from 0 to 2047
Outputs:
- new_master: float32 [2, 2, 2048, 1024], P(None, None, 'dp', 'tensor')
- new_moment_one: float32 [2, 2, 2048, 1024], P(None, None, 'dp', 'tensor')
- new_moment_two: float32 [2, 2, 2048, 1024], P(None, None, 'dp', 'tensor')
The draws below stay inside these ranges and needn't reach their ends.
All inputs are finite; a program needn't handle non-finite values.
Results may differ from the reference program's by a relative error of at most 0.0052.
The reference program's roundings to bfloat16 on the way count: a program that leaves them out, or rounds other values in their place, can miss the bound.
Values may be sent and summed in bfloat16 or wider, within the bound.
A program may use at most 320 MiB of HBM per device.

```python
import math
import jax
import jax.numpy as jnp
from jax import lax

MODEL_WIDTH = 8192
QUERY_HEADS = 32
KEY_VALUE_HEADS = 8
HEAD_SIZE = 128
PREFIX_SLOTS = 2048
TOK_DEV = 256
BLOCKS = 16
TOKEN_COUNT = 4096
N_DP = 16


def row_field_label(key, shape, spread):
    noise = jax.random.normal(jax.random.fold_in(key, 1), shape, jnp.float32)
    scales = jnp.exp(jax.random.uniform(jax.random.fold_in(key, 2), shape[:-2] + (1, 1), jnp.float32, -spread, spread))
    return jnp.clip(noise * scales, -6.0, 6.0)


def rising_field(key, low_scale, high_scale, row_spread):
    noise = jax.random.normal(jax.random.fold_in(key, 1), (TOKEN_COUNT, MODEL_WIDTH), jnp.float32)
    place = jnp.arange(MODEL_WIDTH).astype(jnp.float32) / (MODEL_WIDTH - 1)
    column_scale = jnp.exp(math.log(low_scale) + (math.log(high_scale) - math.log(low_scale)) * place)
    row_scale = jnp.exp(jax.random.uniform(jax.random.fold_in(key, 2), (TOKEN_COUNT, 1), jnp.float32, -row_spread, row_spread))
    return jnp.clip(noise * column_scale[None, :] * row_scale, -6.0, 6.0)


def draw_x_hidden(key, part):
    key = jax.random.fold_in(key, 31)
    field_label = rising_field(key, 0.5, 2.0, 0.0)
    return field_label.astype(jnp.bfloat16)


def draw_queries_upper(key, part):
    key = jax.random.fold_in(key, 11)
    field_label = row_field_label(key, (BLOCKS, TOK_DEV, QUERY_HEADS, HEAD_SIZE), 0.0)
    return field_label.reshape(TOKEN_COUNT, QUERY_HEADS * HEAD_SIZE).astype(jnp.bfloat16)


def draw_queries_lower(key, part):
    key = jax.random.fold_in(key, 12)
    field_label = row_field_label(key, (BLOCKS, TOK_DEV, QUERY_HEADS, HEAD_SIZE), 0.0)
    return field_label.reshape(TOKEN_COUNT, QUERY_HEADS * HEAD_SIZE).astype(jnp.bfloat16)


def draw_prefix_upper(key, part):
    key = jax.random.fold_in(key, 21)
    field_label = row_field_label(key, (2, PREFIX_SLOTS, KEY_VALUE_HEADS, HEAD_SIZE), 0.0)
    return field_label.reshape(2, PREFIX_SLOTS, KEY_VALUE_HEADS * HEAD_SIZE).astype(jnp.bfloat16)


def draw_prefix_lower(key, part):
    key = jax.random.fold_in(key, 22)
    field_label = row_field_label(key, (2, PREFIX_SLOTS, KEY_VALUE_HEADS, HEAD_SIZE), 0.0)
    return field_label.reshape(2, PREFIX_SLOTS, KEY_VALUE_HEADS * HEAD_SIZE).astype(jnp.bfloat16)


def touch_ends(array, rng, least, top_value):
    spot = [jax.random.randint(jax.random.fold_in(rng, axis), (), 0, length) for axis, length in enumerate(array.shape)]
    widest = array.shape.index(max(array.shape))
    beside = spot[:widest] + [(spot[widest] + 1) % array.shape[widest]] + spot[widest + 1:]
    return array.at[tuple(spot)].set(least).at[tuple(beside)].set(top_value)


def levels(key, extent, cuts, least, largest):
    gain = 1.0
    for position, parts in cuts:
        draws = jax.random.uniform(jax.random.fold_in(jax.random.fold_in(key, 6), position), (parts,), jnp.float32, least / len(cuts), largest / len(cuts))
        gain = gain * jnp.repeat(jnp.exp(draws), extent[position] // parts).reshape((-1,) + (1,) * (len(extent) - 1 - position))
    return gain


def scatter_about(key, dims, scale, bound, split=(), kind=jnp.bfloat16):
    array = scale * jax.random.normal(key, dims, jnp.float32)
    if split:
        array = array * levels(key, dims, split, -0.22, 0.18)
    return jnp.clip(array, -bound, bound).astype(kind)


def setup_inputs(seed: int = 0) -> dict:
    streams_of = jax.random.split(jax.random.key(seed), 19)
    x_hidden = draw_x_hidden(jax.random.fold_in(streams_of[18], 71), 0)
    norm_gain = jnp.clip(1.0 + 0.15 * jax.random.normal(streams_of[1], (MODEL_WIDTH,), jnp.float32), 0.25, 1.75).astype(jnp.bfloat16)
    queries_upper = draw_queries_upper(jax.random.fold_in(streams_of[18], 71), 0)
    block_key_value_above = scatter_about(streams_of[3], (2, TOKEN_COUNT, KEY_VALUE_HEADS * HEAD_SIZE), 1.0, 6.0, ((1, 16), (2, 2)))
    out_grad_upper = scatter_about(streams_of[4], (TOKEN_COUNT, QUERY_HEADS * HEAD_SIZE), 1.0, 6.0, ((0, 16), (1, 2)))
    resid_grad = scatter_about(streams_of[5], (TOKEN_COUNT, MODEL_WIDTH), 0.15, 2.0, ((0, 16), (1, 2)))
    queries_lower = draw_queries_lower(jax.random.fold_in(streams_of[18], 71), 0)
    block_key_value_below = scatter_about(streams_of[7], (2, TOKEN_COUNT, KEY_VALUE_HEADS * HEAD_SIZE), 1.0, 6.0, ((1, 16), (2, 2)))
    w_query = scatter_about(streams_of[8], (MODEL_WIDTH, QUERY_HEADS * HEAD_SIZE), MODEL_WIDTH ** -0.5, 0.0625, ((0, 16), (1, 2)))
    key_weight_above = scatter_about(streams_of[9], (MODEL_WIDTH, KEY_VALUE_HEADS * HEAD_SIZE), MODEL_WIDTH ** -0.5, 0.0625, ((0, 16), (1, 2)))
    value_weight_above = scatter_about(streams_of[10], (MODEL_WIDTH, KEY_VALUE_HEADS * HEAD_SIZE), MODEL_WIDTH ** -0.5, 0.0625, ((0, 16), (1, 2)))
    w_output = scatter_about(streams_of[11], (QUERY_HEADS * HEAD_SIZE, MODEL_WIDTH), (QUERY_HEADS * HEAD_SIZE) ** -0.5, 0.09375, ((0, 2), (1, 16)))
    prefix_upper = draw_prefix_upper(jax.random.fold_in(streams_of[18], 71), 0)
    prefix_lower = draw_prefix_lower(jax.random.fold_in(streams_of[18], 71), 0)
    master = scatter_about(streams_of[14], (2, 2, PREFIX_SLOTS, KEY_VALUE_HEADS * HEAD_SIZE), 1.0, 6.0, ((2, 16), (3, 2)), jnp.float32)
    first_moment_state = scatter_about(streams_of[15], (2, 2, PREFIX_SLOTS, KEY_VALUE_HEADS * HEAD_SIZE), 0.003, 0.046875, ((2, 16), (3, 2)), jnp.float32)
    second_moment_state = jnp.clip(jnp.exp(math.log(0.01) - 4.6051702 * jax.random.uniform(streams_of[16], (2, 2, PREFIX_SLOTS, KEY_VALUE_HEADS * HEAD_SIZE), jnp.float32) ** levels(streams_of[16], (2, 2, PREFIX_SLOTS, KEY_VALUE_HEADS * HEAD_SIZE), ((2, 16), (3, 2)), -0.2, 0.2)), 0.0001, 0.01)
    offsets = touch_ends(jax.random.randint(streams_of[17], (BLOCKS,), 0, 2048), jax.random.fold_in(streams_of[17], 1), 0, 2047).astype(jnp.int32)
    return {"x_hidden": x_hidden, "norm_gain": norm_gain, "queries_upper": queries_upper, "block_key_value_above": block_key_value_above, "out_grad_upper": out_grad_upper, "resid_grad": resid_grad, "queries_lower": queries_lower, "block_key_value_below": block_key_value_below, "w_query": w_query, "key_weight_above": key_weight_above, "value_weight_above": value_weight_above, "w_output": w_output, "prefix_upper": prefix_upper, "prefix_lower": prefix_lower, "master": master, "first_moment_state": first_moment_state, "second_moment_state": second_moment_state, "offsets": offsets}


norm_eps = 1e-05
rope_base = 500000.0
adam_rate = 0.05
beta_one = 0.9
beta_two = 0.999
adam_count = 10.0
adam_eps = 1e-08

def attend_back(queries, keys, values, out_grad):
    rows = queries.shape[0]
    key_rows = keys.shape[0]
    kv_heads = keys.shape[1] // HEAD_SIZE
    group = queries.shape[1] // HEAD_SIZE // kv_heads
    scale = HEAD_SIZE ** (-0.5)
    query_f = queries.astype(jnp.float32).reshape(rows, kv_heads, group, HEAD_SIZE)
    key_f = keys.astype(jnp.float32).reshape(key_rows, kv_heads, HEAD_SIZE)
    value_f = values.astype(jnp.float32).reshape(key_rows, kv_heads, HEAD_SIZE)
    grad_f = out_grad.astype(jnp.float32).reshape(rows, kv_heads, group, HEAD_SIZE)
    scores = jnp.einsum('tkgd,ukd->kgtu', query_f, key_f) * scale
    row_ids = jnp.arange(rows)[:, None]
    col_ids = jnp.arange(key_rows)[None, :]
    allowed = (col_ids < PREFIX_SLOTS) | (col_ids - PREFIX_SLOTS <= row_ids)
    scores = jnp.where(allowed, scores, -jnp.inf)
    top = lax.optimization_barrier(jnp.max(scores, axis=-1, keepdims=True))
    expo = jnp.exp(scores - top)
    probs = expo / lax.optimization_barrier(jnp.sum(expo, axis=-1, keepdims=True))
    probs_b = probs.astype(jnp.bfloat16).astype(jnp.float32)
    attn = jnp.einsum('kgtu,ukd->tkgd', probs_b, value_f)
    delta = jnp.transpose(lax.optimization_barrier(jnp.sum(grad_f * attn, axis=-1)), (1, 2, 0))
    dprob = jnp.einsum('tkgd,ukd->kgtu', grad_f, value_f)
    dscore = (probs * (dprob - delta[..., None])).astype(jnp.bfloat16).astype(jnp.float32)
    grad_query = jnp.einsum('kgtu,ukd->tkgd', dscore, key_f) * scale
    grad_key = jnp.einsum('kgtu,tkgd->ukd', dscore, query_f) * scale
    grad_value = jnp.einsum('kgtu,tkgd->ukd', probs_b, grad_f)
    return (grad_query.reshape(rows, -1), grad_key.reshape(key_rows, -1), grad_value.reshape(key_rows, -1))

def rotate_back(grad, positions):
    half = HEAD_SIZE // 2
    shaped = grad.reshape(grad.shape[:-1] + (grad.shape[-1] // HEAD_SIZE, HEAD_SIZE))
    freqs = jnp.exp(-jnp.log(rope_base) * 2.0 * jnp.arange(half).astype(jnp.float32) / HEAD_SIZE)
    angle = positions[..., None, None] * freqs
    cosine = jnp.cos(angle)
    sine = jnp.sin(angle)
    first = shaped[..., :half]
    second = shaped[..., half:]
    out_first = first * cosine + second * sine
    out_second = second * cosine - first * sine
    return jnp.concatenate([out_first, out_second], axis=-1).reshape(grad.shape)

def layer_back(queries, block_kv, prefix, out_grad):
    width = prefix.shape[2]

    def step_block(carry, items):
        query_blk, key_blk, value_blk, grad_blk = items
        keys = jnp.concatenate([prefix[0], key_blk], axis=0)
        values = jnp.concatenate([prefix[1], value_blk], axis=0)
        grad_query, grad_key, grad_value = attend_back(query_blk, keys, values, grad_blk)
        carry = (carry[0] + grad_key[:PREFIX_SLOTS], carry[1] + grad_value[:PREFIX_SLOTS])
        return (carry, (grad_query, grad_key[PREFIX_SLOTS:], grad_value[PREFIX_SLOTS:]))
    zero_acc = jnp.zeros((PREFIX_SLOTS, width), jnp.float32)
    items = (queries.reshape(N_DP, TOK_DEV, -1), block_kv[0].reshape(N_DP, TOK_DEV, -1), block_kv[1].reshape(N_DP, TOK_DEV, -1), out_grad.reshape(N_DP, TOK_DEV, -1))
    return lax.scan(step_block, (zero_acc, zero_acc), items)

def reference(x_hidden, norm_gain, queries_upper, block_key_value_above, out_grad_upper, resid_grad, queries_lower, block_key_value_below, w_query, key_weight_above, value_weight_above, w_output, prefix_upper, prefix_lower, master, first_moment_state, second_moment_state, offsets):
    (upper_key, upper_value), (grad_query, grad_key, grad_value) = layer_back(queries_upper, block_key_value_above, prefix_upper, out_grad_upper)
    positions = (PREFIX_SLOTS + offsets[:, None] + jnp.arange(TOK_DEV)[None, :]).astype(jnp.float32)
    query_rot = rotate_back(grad_query, positions).astype(jnp.bfloat16).reshape(N_DP * TOK_DEV, -1)
    key_rot = rotate_back(grad_key, positions).astype(jnp.bfloat16).reshape(N_DP * TOK_DEV, -1)
    value_rot = grad_value.astype(jnp.bfloat16).reshape(N_DP * TOK_DEV, -1)
    hidden_grad = jnp.dot(query_rot, w_query.T, preferred_element_type=jnp.float32)
    hidden_grad = hidden_grad + jnp.dot(key_rot, key_weight_above.T, preferred_element_type=jnp.float32)
    hidden_grad = hidden_grad + jnp.dot(value_rot, value_weight_above.T, preferred_element_type=jnp.float32)
    hidden_f = x_hidden.astype(jnp.float32)
    recip = 1.0 / jnp.sqrt(lax.optimization_barrier(jnp.mean(hidden_f * hidden_f, axis=-1, keepdims=True)) + norm_eps)
    gained = norm_gain.astype(jnp.float32) * hidden_grad
    cross = lax.optimization_barrier(jnp.mean(hidden_f * gained, axis=-1, keepdims=True))
    grad_hidden = resid_grad.astype(jnp.float32) + recip * gained - hidden_f * recip ** 3 * cross
    grad_hidden = grad_hidden.astype(jnp.bfloat16)
    out_grad_lower = jnp.dot(grad_hidden, w_output.T, preferred_element_type=jnp.float32).astype(jnp.bfloat16)
    (lower_key, lower_value), unused = layer_back(queries_lower, block_key_value_below, prefix_lower, out_grad_lower)
    grads = jnp.stack([jnp.stack([lower_key, lower_value]), jnp.stack([upper_key, upper_value])])
    new_moment_one = beta_one * first_moment_state + (1.0 - beta_one) * grads
    new_moment_two = beta_two * second_moment_state + (1.0 - beta_two) * grads * grads
    first_hat = new_moment_one / (1.0 - beta_one ** adam_count)
    second_hat = new_moment_two / (1.0 - beta_two ** adam_count)
    new_master = master - adam_rate * first_hat / (jnp.sqrt(second_hat) + adam_eps)
    return (new_master, new_moment_one, new_moment_two)
```

```python
import functools

import jax
import jax.numpy as jnp
from jax import lax
from jax.experimental import pallas as pl
from jax.experimental.pallas import tpu as pltpu
from jax.sharding import PartitionSpec as P

MODEL_WIDTH = 8192
HEAD_SIZE = 128
PREFIX_SLOTS = 2048
CHUNK = 256


norm_eps = 1e-05
rope_base = 500000.0
adam_rate = 0.05
beta_one = 0.9
beta_two = 0.999
adam_count = 10.0
adam_eps = 1e-08


def attend_kernel(with_query, query_ref, grad_ref, block_ref, prefix_ref, *rest):
    if with_query:
        key_out, value_out, own_key_out, own_value_out, query_out, score_ref, dprob_ref = rest
    else:
        key_out, value_out, score_ref, dprob_ref = rest
    tokens = query_ref.shape[0]
    slots = prefix_ref.shape[1]
    step = min(CHUNK, slots)
    scale = HEAD_SIZE ** (-0.5)
    spans = [(True, i, step) for i in range(0, slots, step)] + [(False, 0, tokens)]
    query = query_ref[...]
    grad = grad_ref[...]

    def rows(which, span):
        prefix_part, start, size = span
        ref = prefix_ref if prefix_part else block_ref
        return ref[which, start : start + size, :]

    def place(span):
        prefix_part, start, size = span
        first = start if prefix_part else slots
        return slice(first, first + size)

    contract_last = (((1,), (1,)), ((), ()))
    top = jnp.full((1, tokens), -jnp.inf, jnp.float32)
    for span in spans:
        score = (
            lax.dot_general(rows(0, span), query, contract_last, preferred_element_type=jnp.float32)
            * scale
        )
        if not span[0]:
            key_ids = lax.broadcasted_iota(jnp.int32, score.shape, 0)
            token_ids = lax.broadcasted_iota(jnp.int32, score.shape, 1)
            score = jnp.where(key_ids <= token_ids, score, -jnp.inf)
        score_ref[place(span), :] = score
        top = jnp.maximum(top, jnp.max(score, axis=0, keepdims=True))
    total = jnp.zeros((1, tokens), jnp.float32)
    for span in spans:
        expo = jnp.exp(score_ref[place(span), :] - top)
        score_ref[place(span), :] = expo
        total = total + jnp.sum(expo, axis=0, keepdims=True)
    inverse = 1.0 / total
    first_head = pl.program_id(1) == 0

    def add(ref, start, size, value):
        @pl.when(first_head)
        def _():
            ref[start : start + size, :] = value

        @pl.when(jnp.logical_not(first_head))
        def _():
            ref[start : start + size, :] += value

    delta = jnp.zeros((1, tokens), jnp.float32)
    for span in spans:
        probs = score_ref[place(span), :] * inverse
        score_ref[place(span), :] = probs
        probs_b = probs.astype(jnp.bfloat16)
        dprob = lax.dot_general(
            rows(1, span), grad, contract_last, preferred_element_type=jnp.float32
        )
        dprob_ref[place(span), :] = dprob
        delta = delta + jnp.sum(probs_b.astype(jnp.float32) * dprob, axis=0, keepdims=True)
        if span[0] or with_query:
            ref = value_out if span[0] else own_value_out
            part = jnp.dot(probs_b, grad, preferred_element_type=jnp.float32)
            add(ref, span[1], span[2], part)
    if with_query:
        grad_query = jnp.zeros((HEAD_SIZE, tokens), jnp.float32)
    for span in spans:
        if not (span[0] or with_query):
            continue
        dscore = (score_ref[place(span), :] * (dprob_ref[place(span), :] - delta)).astype(
            jnp.bfloat16
        )
        ref = key_out if span[0] else own_key_out
        part = jnp.dot(dscore, query, preferred_element_type=jnp.float32) * scale
        add(ref, span[1], span[2], part)
        if with_query:
            grad_query = grad_query + lax.dot_general(
                rows(0, span), dscore, (((0,), (0,)), ((), ())), preferred_element_type=jnp.float32
            )
    if with_query:
        query_out[...] = grad_query.T * scale


def layer_back(queries, block_kv, prefix, out_grad, with_query):
    tokens, width = queries.shape
    slots, kv_width = prefix.shape[1:]
    kv_heads = kv_width // HEAD_SIZE
    group = width // kv_width
    head_spec = pl.BlockSpec((tokens, HEAD_SIZE), lambda k, g: (0, k * group + g))
    own_spec = pl.BlockSpec((tokens, HEAD_SIZE), lambda k, g: (0, k))
    slot_spec = pl.BlockSpec((slots, HEAD_SIZE), lambda k, g: (0, k))
    f32 = jnp.float32
    out_shape = [jax.ShapeDtypeStruct((slots, kv_width), f32)] * 2
    out_specs = [slot_spec] * 2
    if with_query:
        out_shape += [jax.ShapeDtypeStruct((tokens, kv_width), f32)] * 2
        out_shape += [jax.ShapeDtypeStruct((tokens, width), f32)]
        out_specs += [own_spec] * 2 + [head_spec]
    matmuls = 5 if with_query else 4
    keys = slots + tokens
    return pl.pallas_call(
        functools.partial(attend_kernel, with_query),
        grid=(kv_heads, group),
        in_specs=[
            head_spec,
            head_spec,
            pl.BlockSpec((2, tokens, HEAD_SIZE), lambda k, g: (0, 0, k)),
            pl.BlockSpec((2, slots, HEAD_SIZE), lambda k, g: (0, 0, k)),
        ],
        out_shape=out_shape,
        out_specs=out_specs,
        scratch_shapes=[pltpu.VMEM((keys, tokens), f32), pltpu.VMEM((keys, tokens), f32)],
        compiler_params=pltpu.CompilerParams(
            dimension_semantics=("arbitrary", "arbitrary"), vmem_limit_bytes=40 * 2**20
        ),
        cost_estimate=pl.CostEstimate(
            flops=2 * matmuls * tokens * keys * width,
            bytes_accessed=20 * 2**20,
            transcendentals=tokens * keys * width // HEAD_SIZE,
        ),
        name="attend_upper" if with_query else "attend_lower",
    )(queries, out_grad, block_kv, prefix)


def rotate_back(grad, positions):
    half = HEAD_SIZE // 2
    shaped = grad.reshape(grad.shape[:-1] + (grad.shape[-1] // HEAD_SIZE, HEAD_SIZE))
    freqs = jnp.exp(-jnp.log(rope_base) * 2.0 * jnp.arange(half).astype(jnp.float32) / HEAD_SIZE)
    angle = positions[..., None, None] * freqs
    cosine = jnp.cos(angle)
    sine = jnp.sin(angle)
    first = shaped[..., :half]
    second = shaped[..., half:]
    out_first = first * cosine + second * sine
    out_second = second * cosine - first * sine
    return jnp.concatenate([out_first, out_second], axis=-1).reshape(grad.shape)


def share(grads):
    return [lax.psum_scatter(g, "dp", scatter_dimension=0, tiled=True) for g in grads]


def per_device(
    x_hidden,
    norm_gain,
    queries_upper,
    block_key_value_above,
    out_grad_upper,
    resid_grad,
    queries_lower,
    block_key_value_below,
    w_query,
    key_weight_above,
    value_weight_above,
    w_output,
    prefix_upper,
    prefix_lower,
    master,
    first_moment_state,
    second_moment_state,
    offsets,
):
    tokens = queries_upper.shape[0]
    upper_key, upper_value, own_key, own_value, grad_query = layer_back(
        queries_upper, block_key_value_above, prefix_upper, out_grad_upper, True
    )
    positions = (PREFIX_SLOTS + offsets[0] + jnp.arange(tokens)).astype(jnp.float32)
    query_rot = rotate_back(grad_query, positions).astype(jnp.bfloat16)
    key_rot = rotate_back(own_key, positions).astype(jnp.bfloat16)
    value_rot = own_value.astype(jnp.bfloat16)
    columns = jnp.einsum(
        "tc,nc->tn",
        query_rot,
        lax.all_gather(w_query, "dp", axis=0, tiled=True),
        preferred_element_type=jnp.float32,
    )
    columns = columns + jnp.einsum(
        "tc,nc->tn",
        key_rot,
        lax.all_gather(key_weight_above, "dp", axis=0, tiled=True),
        preferred_element_type=jnp.float32,
    )
    columns = columns + jnp.einsum(
        "tc,nc->tn",
        value_rot,
        lax.all_gather(value_weight_above, "dp", axis=0, tiled=True),
        preferred_element_type=jnp.float32,
    )
    partial_grad = columns
    hidden_grad = lax.psum_scatter(partial_grad, "tensor", scatter_dimension=1, tiled=True)
    hidden_f = x_hidden.astype(jnp.float32)
    gained = norm_gain.astype(jnp.float32) * hidden_grad
    square_sum, cross_sum = lax.psum(
        (jnp.sum(hidden_f * hidden_f, axis=-1), jnp.sum(hidden_f * gained, axis=-1)), "tensor"
    )
    recip = 1.0 / jnp.sqrt(square_sum[:, None] / MODEL_WIDTH + norm_eps)
    cross = cross_sum[:, None] / MODEL_WIDTH
    grad_local = resid_grad.astype(jnp.float32) + recip * gained - hidden_f * recip**3 * cross
    grad_hidden = lax.all_gather(grad_local.astype(jnp.bfloat16), "tensor", axis=1, tiled=True)
    columns = grad_hidden
    out_grad_lower = jnp.einsum(
        "td,hd->th",
        columns,
        lax.all_gather(w_output, "dp", axis=1, tiled=True),
        preferred_element_type=jnp.float32,
    ).astype(jnp.bfloat16)
    lower_key, lower_value = layer_back(
        queries_lower, block_key_value_below, prefix_lower, out_grad_lower, False
    )
    upper_key, upper_value = share((upper_key, upper_value))
    lower_key, lower_value = share((lower_key, lower_value))
    own_grads = jnp.stack(
        [jnp.stack([lower_key, lower_value]), jnp.stack([upper_key, upper_value])]
    )
    new_moment_one = beta_one * first_moment_state + (1.0 - beta_one) * own_grads
    new_moment_two = beta_two * second_moment_state + (1.0 - beta_two) * own_grads * own_grads
    first_hat = new_moment_one / (1.0 - beta_one**adam_count)
    second_hat = new_moment_two / (1.0 - beta_two**adam_count)
    new_master = master - adam_rate * first_hat / (jnp.sqrt(second_hat) + adam_eps)
    return (new_master, new_moment_one, new_moment_two)


def solution(mesh):
    return jax.shard_map(
        per_device,
        mesh=mesh,
        in_specs=(
            P("dp", "tensor"),
            P("tensor"),
            P("dp", "tensor"),
            P(None, "dp", "tensor"),
            P("dp", "tensor"),
            P("dp", "tensor"),
            P("dp", "tensor"),
            P(None, "dp", "tensor"),
            P("dp", "tensor"),
            P("dp", "tensor"),
            P("dp", "tensor"),
            P("tensor", "dp"),
            P(None, None, "tensor"),
            P(None, None, "tensor"),
            P(None, None, "dp", "tensor"),
            P(None, None, "dp", "tensor"),
            P(None, None, "dp", "tensor"),
            P("dp"),
        ),
        out_specs=(
            P(None, None, "dp", "tensor"),
            P(None, None, "dp", "tensor"),
            P(None, None, "dp", "tensor"),
        ),
        check_vma=False,
    )
```

```python
import functools

import jax
import jax.numpy as jnp
from jax import lax
from jax.experimental import pallas as pl
from jax.experimental.pallas import tpu as pltpu
from jax.sharding import PartitionSpec as P

MODEL_WIDTH = 8192
HEAD_SIZE = 128
PREFIX_SLOTS = 2048
CHUNK = 256


norm_eps = 1e-05
rope_base = 500000.0
adam_rate = 0.05
beta_one = 0.9
beta_two = 0.999
adam_count = 10.0
adam_eps = 1e-08


def attend_kernel(with_query, query_ref, grad_ref, block_ref, prefix_ref, *rest):
    if with_query:
        key_out, value_out, own_key_out, own_value_out, query_out, score_ref, dprob_ref = rest
    else:
        key_out, value_out, score_ref, dprob_ref = rest
    tokens = query_ref.shape[0]
    slots = prefix_ref.shape[1]
    step = min(CHUNK, slots)
    scale = HEAD_SIZE ** (-0.5)
    spans = [(True, i, step) for i in range(0, slots, step)] + [(False, 0, tokens)]
    query = query_ref[...]
    grad = grad_ref[...]

    def rows(which, span):
        prefix_part, start, size = span
        ref = prefix_ref if prefix_part else block_ref
        return ref[which, start : start + size, :]

    def place(span):
        prefix_part, start, size = span
        first = start if prefix_part else slots
        return slice(first, first + size)

    contract_last = (((1,), (1,)), ((), ()))
    top = jnp.full((1, tokens), -jnp.inf, jnp.float32)
    for span in spans:
        score = (
            lax.dot_general(rows(0, span), query, contract_last, preferred_element_type=jnp.float32)
            * scale
        )
        if not span[0]:
            key_ids = lax.broadcasted_iota(jnp.int32, score.shape, 0)
            token_ids = lax.broadcasted_iota(jnp.int32, score.shape, 1)
            score = jnp.where(key_ids <= token_ids, score, -jnp.inf)
        score_ref[place(span), :] = score
        top = jnp.maximum(top, jnp.max(score, axis=0, keepdims=True))
    total = jnp.zeros((1, tokens), jnp.float32)
    for span in spans:
        expo = jnp.exp(score_ref[place(span), :] - top)
        score_ref[place(span), :] = expo
        total = total + jnp.sum(expo, axis=0, keepdims=True)
    inverse = 1.0 / total
    first_head = pl.program_id(1) == 0

    def add(ref, start, size, value):
        @pl.when(first_head)
        def _():
            ref[start : start + size, :] = value

        @pl.when(jnp.logical_not(first_head))
        def _():
            ref[start : start + size, :] += value

    delta = jnp.zeros((1, tokens), jnp.float32)
    for span in spans:
        probs = score_ref[place(span), :] * inverse
        score_ref[place(span), :] = probs
        probs_b = probs.astype(jnp.bfloat16)
        dprob = lax.dot_general(
            rows(1, span), grad, contract_last, preferred_element_type=jnp.float32
        )
        dprob_ref[place(span), :] = dprob
        delta = delta + jnp.sum(probs_b.astype(jnp.float32) * dprob, axis=0, keepdims=True)
        if span[0] or with_query:
            ref = value_out if span[0] else own_value_out
            part = jnp.dot(probs_b, grad, preferred_element_type=jnp.float32)
            add(ref, span[1], span[2], part)
    if with_query:
        grad_query = jnp.zeros((HEAD_SIZE, tokens), jnp.float32)
    for span in spans:
        if not (span[0] or with_query):
            continue
        dscore = (score_ref[place(span), :] * (dprob_ref[place(span), :] - delta)).astype(
            jnp.bfloat16
        )
        ref = key_out if span[0] else own_key_out
        part = jnp.dot(dscore, query, preferred_element_type=jnp.float32) * scale
        add(ref, span[1], span[2], part)
        if with_query:
            grad_query = grad_query + lax.dot_general(
                rows(0, span), dscore, (((0,), (0,)), ((), ())), preferred_element_type=jnp.float32
            )
    if with_query:
        query_out[...] = grad_query.T * scale


def layer_back(queries, block_kv, prefix, out_grad, with_query):
    tokens, width = queries.shape
    slots, kv_width = prefix.shape[1:]
    kv_heads = kv_width // HEAD_SIZE
    group = width // kv_width
    head_spec = pl.BlockSpec((tokens, HEAD_SIZE), lambda k, g: (0, k * group + g))
    own_spec = pl.BlockSpec((tokens, HEAD_SIZE), lambda k, g: (0, k))
    slot_spec = pl.BlockSpec((slots, HEAD_SIZE), lambda k, g: (0, k))
    f32 = jnp.float32
    out_shape = [jax.ShapeDtypeStruct((slots, kv_width), f32)] * 2
    out_specs = [slot_spec] * 2
    if with_query:
        out_shape += [jax.ShapeDtypeStruct((tokens, kv_width), f32)] * 2
        out_shape += [jax.ShapeDtypeStruct((tokens, width), f32)]
        out_specs += [own_spec] * 2 + [head_spec]
    matmuls = 5 if with_query else 4
    keys = slots + tokens
    return pl.pallas_call(
        functools.partial(attend_kernel, with_query),
        grid=(kv_heads, group),
        in_specs=[
            head_spec,
            head_spec,
            pl.BlockSpec((2, tokens, HEAD_SIZE), lambda k, g: (0, 0, k)),
            pl.BlockSpec((2, slots, HEAD_SIZE), lambda k, g: (0, 0, k)),
        ],
        out_shape=out_shape,
        out_specs=out_specs,
        scratch_shapes=[pltpu.VMEM((keys, tokens), f32), pltpu.VMEM((keys, tokens), f32)],
        compiler_params=pltpu.CompilerParams(
            dimension_semantics=("arbitrary", "arbitrary"), vmem_limit_bytes=40 * 2**20
        ),
        cost_estimate=pl.CostEstimate(
            flops=2 * matmuls * tokens * keys * width,
            bytes_accessed=20 * 2**20,
            transcendentals=tokens * keys * width // HEAD_SIZE,
        ),
        name="attend_upper" if with_query else "attend_lower",
    )(queries, out_grad, block_kv, prefix)


def rotate_back(grad, positions):
    half = HEAD_SIZE // 2
    shaped = grad.reshape(grad.shape[:-1] + (grad.shape[-1] // HEAD_SIZE, HEAD_SIZE))
    freqs = jnp.exp(-jnp.log(rope_base) * 2.0 * jnp.arange(half).astype(jnp.float32) / HEAD_SIZE)
    angle = positions[..., None, None] * freqs
    cosine = jnp.cos(angle)
    sine = jnp.sin(angle)
    first = shaped[..., :half]
    second = shaped[..., half:]
    out_first = first * cosine + second * sine
    out_second = second * cosine - first * sine
    return jnp.concatenate([out_first, out_second], axis=-1).reshape(grad.shape)


def share(grads):
    both = jnp.concatenate(grads, axis=1)
    mine = lax.psum_scatter(both, "dp", scatter_dimension=0, tiled=True)
    return jnp.split(mine, len(grads), axis=1)


def exchange_sum(values, axis):
    size, me = lax.axis_size(axis), lax.axis_index(axis)
    width = values.shape[1] // size

    def part(owner):
        return lax.dynamic_slice_in_dim(values, owner * width, width, 1)

    total = part(me)
    for step in range(1, size):
        pairs = [(i, (i + step) % size) for i in range(size)]
        total = total + lax.ppermute(part((me + step) % size), axis, pairs)
    return total


def exchange_whole(part, axis):
    size, me = lax.axis_size(axis), lax.axis_index(axis)
    width = part.shape[1]
    whole = jnp.zeros((part.shape[0], width * size), part.dtype)
    whole = lax.dynamic_update_slice_in_dim(whole, part, me * width, 1)
    for step in range(1, size):
        pairs = [(i, (i + step) % size) for i in range(size)]
        owner = (me - step + size) % size
        got = lax.ppermute(part, axis, pairs)
        whole = lax.dynamic_update_slice_in_dim(whole, got, owner * width, 1)
    return whole


def per_device(
    x_hidden,
    norm_gain,
    queries_upper,
    block_key_value_above,
    out_grad_upper,
    resid_grad,
    queries_lower,
    block_key_value_below,
    w_query,
    key_weight_above,
    value_weight_above,
    w_output,
    prefix_upper,
    prefix_lower,
    master,
    first_moment_state,
    second_moment_state,
    offsets,
):
    tokens = queries_upper.shape[0]
    upper_key, upper_value, own_key, own_value, grad_query = layer_back(
        queries_upper, block_key_value_above, prefix_upper, out_grad_upper, True
    )
    positions = (PREFIX_SLOTS + offsets[0] + jnp.arange(tokens)).astype(jnp.float32)
    query_rot = rotate_back(grad_query, positions).astype(jnp.bfloat16)
    key_rot = rotate_back(own_key, positions).astype(jnp.bfloat16)
    value_rot = own_value.astype(jnp.bfloat16)
    weights = jnp.concatenate([w_query, key_weight_above, value_weight_above], axis=1)
    partial_grad = jnp.einsum(
        "tc,nc->tn",
        jnp.concatenate([query_rot, key_rot, value_rot], axis=1),
        lax.all_gather(weights, "dp", axis=0, tiled=True),
        preferred_element_type=jnp.float32,
    )
    hidden_grad = exchange_sum(partial_grad, "tensor")
    hidden_f = x_hidden.astype(jnp.float32)
    gained = norm_gain.astype(jnp.float32) * hidden_grad
    square_sum, cross_sum = lax.psum(
        (jnp.sum(hidden_f * hidden_f, axis=-1), jnp.sum(hidden_f * gained, axis=-1)), "tensor"
    )
    recip = 1.0 / jnp.sqrt(square_sum[:, None] / MODEL_WIDTH + norm_eps)
    cross = cross_sum[:, None] / MODEL_WIDTH
    grad_local = resid_grad.astype(jnp.float32) + recip * gained - hidden_f * recip**3 * cross
    grad_hidden = exchange_whole(grad_local.astype(jnp.bfloat16), "tensor")
    columns = grad_hidden
    out_grad_lower = jnp.einsum(
        "td,hd->th",
        columns,
        lax.all_gather(w_output, "dp", axis=1, tiled=True),
        preferred_element_type=jnp.float32,
    ).astype(jnp.bfloat16)
    lower_key, lower_value = layer_back(
        queries_lower, block_key_value_below, prefix_lower, out_grad_lower, False
    )
    upper_key, upper_value = share((upper_key, upper_value))
    lower_key, lower_value = share((lower_key, lower_value))
    own_grads = jnp.stack(
        [jnp.stack([lower_key, lower_value]), jnp.stack([upper_key, upper_value])]
    )
    new_moment_one = beta_one * first_moment_state + (1.0 - beta_one) * own_grads
    new_moment_two = beta_two * second_moment_state + (1.0 - beta_two) * own_grads * own_grads
    first_hat = new_moment_one / (1.0 - beta_one**adam_count)
    second_hat = new_moment_two / (1.0 - beta_two**adam_count)
    new_master = master - adam_rate * first_hat / (jnp.sqrt(second_hat) + adam_eps)
    return (new_master, new_moment_one, new_moment_two)


def solution(mesh):
    return jax.shard_map(
        per_device,
        mesh=mesh,
        in_specs=(
            P("dp", "tensor"),
            P("tensor"),
            P("dp", "tensor"),
            P(None, "dp", "tensor"),
            P("dp", "tensor"),
            P("dp", "tensor"),
            P("dp", "tensor"),
            P(None, "dp", "tensor"),
            P("dp", "tensor"),
            P("dp", "tensor"),
            P("dp", "tensor"),
            P("tensor", "dp"),
            P(None, None, "tensor"),
            P(None, None, "tensor"),
            P(None, None, "dp", "tensor"),
            P(None, None, "dp", "tensor"),
            P(None, None, "dp", "tensor"),
            P("dp"),
        ),
        out_specs=(
            P(None, None, "dp", "tensor"),
            P(None, None, "dp", "tensor"),
            P(None, None, "dp", "tensor"),
        ),
        check_vma=False,
    )
```
